512 devices in a mesh: inp: 32 (over z_lo, x), tm: 16 (over z_hi, y, core).
Axes of the slice: x: 4, y: 4, z: 16 (z_hi: 2, z_lo: 8; z = z_hi * 8 + z_lo), core: 2. Of those that a mesh axis runs over, the one named last changes fastest.
Arguments:
- voltages: bfloat16 [1024, 524288], P('inp', 'tm'), may hold values from -400 to 400, as said below
Outputs:
- visibilities: bfloat16 [512, 1024, 1024], P(('inp', 'tm'))
The draws below stay inside these ranges and needn't reach their ends.
Inputs may be any that keep to these rules, and one draw needn't show every extreme that they name: `voltages`: magnitudes stay within about 400.
All inputs are finite; a program needn't handle non-finite values.
Results may differ from the reference program's by a relative error of at most 0.0034.
Values may be sent and summed in bfloat16 or wider, within the bound.
No kernel may reach another device: no remote copies, remote signals or barrier semaphores. Data moves between devices by JAX's collectives and lax.ppermute only.
A program may use at most 64 MiB of HBM per device.

```python
import math
import jax
import jax.numpy as jnp
from jax import lax

INPUTS = 1024
NFFT = 2048
CHANNELS = 512
TAPS = 4
NSPEC = 256


def draw_voltages(key, part):
    key = jax.random.fold_in(key, 7)
    key_list = jax.random.split(key, 5)
    scales = jnp.exp(jax.random.uniform(key_list[0], (INPUTS, 1, 1), minval=0.0, maxval=math.log(10.0)))
    noise = jnp.clip(jax.random.normal(key_list[1], (INPUTS, NSPEC, NFFT)), -4.0, 4.0)
    mixing = jax.random.uniform(key_list[2], (INPUTS, 2, 1, 1), minval=-0.8, maxval=0.8)
    sources = jnp.clip(jax.random.normal(key_list[3], (2, NSPEC, NFFT)), -4.0, 4.0)
    envelope = jnp.exp(jax.random.uniform(key_list[4], (1, NSPEC, 1), minval=0.0, maxval=math.log(3.0)))
    signal = mixing[:, 0] * sources[0] + mixing[:, 1] * sources[1] + 0.6 * noise
    return (scales * envelope * signal).reshape(INPUTS, NSPEC * NFFT).astype(jnp.bfloat16)


def setup_inputs(seed: int = 0) -> dict:
    streams_of = jax.random.split(jax.random.key(seed), 2)
    voltages = draw_voltages(jax.random.fold_in(streams_of[1], 71), 0)
    return {"voltages": voltages}


def filter_window(tap_count, length):
    sample = jnp.arange(tap_count * length, dtype=jnp.float32) + 0.5
    shaped = jnp.sinc(sample / length - tap_count / 2.0)
    tapered = 0.5 - 0.5 * jnp.cos(2.0 * math.pi * sample / (tap_count * length))
    return (shaped * tapered).reshape(tap_count, length)

def phase_table(length, channels):
    sample = jnp.arange(length, dtype=jnp.int32)
    bin_index = length // 2 - channels + jnp.arange(channels, dtype=jnp.int32)
    product = sample[:, None] * bin_index[None, :] % length
    phase_angle = product.astype(jnp.float32) * (2.0 * math.pi / length)
    paired = jnp.stack([jnp.cos(phase_angle), -jnp.sin(phase_angle)], axis=2)
    return paired.reshape(length, 2 * channels).astype(jnp.bfloat16)

def reference(voltages):
    window = filter_window(TAPS, NFFT)
    table_values = phase_table(NFFT, CHANNELS)
    groups = voltages.reshape(INPUTS // 64, 64, NSPEC * NFFT)

    def one_group(group_rows):
        padded = jnp.concatenate([jnp.zeros((64, (TAPS - 1) * NFFT), jnp.bfloat16), group_rows], axis=1)
        padded = padded.reshape(64, NSPEC + TAPS - 1, NFFT).astype(jnp.float32)
        filtered = window[0] * padded[:, 0:NSPEC, :]
        for tap_index in range(1, TAPS):
            filtered = filtered + window[tap_index] * padded[:, tap_index:tap_index + NSPEC, :]
        filtered = filtered.astype(jnp.bfloat16).reshape(64 * NSPEC, NFFT)
        return jnp.dot(filtered, table_values, preferred_element_type=jnp.float32).astype(jnp.bfloat16)
    spectra = lax.map(one_group, groups)
    spectra = spectra.reshape(INPUTS, NSPEC, CHANNELS, 2).transpose(2, 3, 1, 0)
    upper_mask = jnp.arange(INPUTS)[:, None] <= jnp.arange(INPUTS)[None, :]

    def one_channel(channel_data):
        real_part = channel_data[0]
        imag_part = channel_data[1]
        cross_re = jnp.dot(real_part.T, real_part, preferred_element_type=jnp.float32) + jnp.dot(imag_part.T, imag_part, preferred_element_type=jnp.float32)
        cross_im = jnp.dot(imag_part.T, real_part, preferred_element_type=jnp.float32) - jnp.dot(real_part.T, imag_part, preferred_element_type=jnp.float32)
        mean_power = jnp.diagonal(cross_re) / NSPEC
        gain_values = 1.0 / jnp.sqrt(mean_power + 1e-06)
        packed = jnp.where(upper_mask, cross_re, cross_im)
        return (packed * gain_values[:, None] * gain_values[None, :] / NSPEC).astype(jnp.bfloat16)
    return lax.map(one_channel, spectra)
```

```python
import math

import jax
import jax.numpy as jnp
import ml_dtypes
import numpy as np
from jax import lax
from jax.experimental import pallas as pl
from jax.experimental.pallas import tpu as pltpu
from jax.sharding import PartitionSpec as P

NFFT = 2048
CHANNELS = 512
TAPS = 4
LANES = 128


def filter_window():
    sample = np.arange(TAPS * NFFT, dtype=np.float64) + 0.5
    shaped = np.sinc(sample / NFFT - TAPS / 2.0)
    tapered = 0.5 - 0.5 * np.cos(2.0 * math.pi * sample / (TAPS * NFFT))
    return (shaped * tapered).reshape(TAPS, NFFT).astype(np.float32)


def phase_rows(block):
    sample = np.arange(NFFT, dtype=np.int64)
    bin_index = NFFT // 2 - CHANNELS + np.arange(CHANNELS, dtype=np.int64)
    product = (bin_index[:, None] * sample[None, :]) % NFFT
    angle = (product.astype(np.float32) * np.float32(2.0 * math.pi / NFFT)).astype(np.float64)
    paired = np.stack([np.cos(angle), -np.sin(angle)]).astype(np.float32)
    paired = paired.reshape(2, CHANNELS // block, block, NFFT).transpose(1, 0, 2, 3)
    return paired.reshape(2 * CHANNELS, NFFT).astype(ml_dtypes.bfloat16)


def front_kernel(spec_local, slots, v_ref, w_ref, tab_ref, out_ref, filt, stage):
    inputs = v_ref.shape[0]
    block = tab_ref.shape[0] // 2
    tiles = slots * inputs // LANES

    @pl.when(pl.program_id(0) == 0)
    def _():
        @pl.loop(0, NFFT // LANES)
        def _(q):
            off = pl.multiple_of(q * LANES, LANES)
            weights = [w_ref[k : k + 1, pl.ds(off, LANES)] for k in range(TAPS)]
            rows = [
                v_ref[:, pl.ds(pl.multiple_of(s * NFFT + off, LANES), LANES)].astype(jnp.float32)
                for s in range(spec_local)
            ]
            for j in range(slots):
                total = None
                for k in range(TAPS):
                    s = j + k - TAPS + 1
                    if 0 <= s < spec_local:
                        term = weights[k] * rows[s]
                        total = term if total is None else total + term
                if total is None:
                    total = jnp.zeros((inputs, LANES), jnp.float32)
                filt[j * inputs : (j + 1) * inputs, pl.ds(off, LANES)] = total.astype(jnp.bfloat16)

    acc = lax.dot_general(
        tab_ref[...], filt[...], (((1,), (1,)), ((), ())), preferred_element_type=jnp.float32
    )
    for t in range(tiles):
        for r in range(2):
            stage[pl.ds(2 * t + r, block, stride=2 * tiles), :] = acc[
                r * block : (r + 1) * block, t * LANES : (t + 1) * LANES
            ]
    out_ref[...] = stage[...].astype(jnp.bfloat16)


def back_kernel(groups, total_spectra, x_ref, fold_ref, perm_ref, out_ref, a_ref, at_ref, bt_ref, stage, sems):
    per_group = LANES * 4
    inputs = groups * LANES
    depth = a_ref.shape[0]
    half_sign = jnp.where(lax.broadcasted_iota(jnp.int32, (1, LANES), 1) < LANES // 2, 1.0, -1.0)
    for g in range(groups):
        joined = jnp.concatenate([x_ref[4 * g + i] for i in range(4)], axis=1)
        spectra = jnp.dot(fold_ref[...], joined, preferred_element_type=jnp.float32).astype(jnp.bfloat16)
        turned = jnp.dot(spectra, perm_ref[...], preferred_element_type=jnp.float32).astype(jnp.bfloat16)
        flipped = lax.dot_general(
            perm_ref[...], spectra, (((1,), (1,)), ((), ())), preferred_element_type=jnp.float32
        )
        swapped = pltpu.roll(flipped, LANES // 2, 1) * half_sign
        flipped = flipped.astype(jnp.bfloat16)
        swapped = swapped.astype(jnp.bfloat16)
        for u in range(4):
            rows = slice(u * LANES, (u + 1) * LANES)
            cols = slice(g * LANES, (g + 1) * LANES)
            a_ref[rows, cols] = turned[:, rows]
            at_ref[cols, rows] = flipped[rows, :]
            bt_ref[cols, rows] = swapped[rows, :]
    scale = 1.0 / total_spectra
    wide = a_ref[...].astype(jnp.float32)
    row_gain = lax.rsqrt(jnp.sum(wide * wide, axis=0, keepdims=True) * scale + 1e-06) * scale
    size = inputs // 4
    copies = []
    for i in range(4):
        rows = slice(i * size, (i + 1) * size)
        tall = at_ref[rows, :].astype(jnp.float32)
        col_gain = lax.rsqrt(jnp.sum(tall * tall, axis=1, keepdims=True) * scale + 1e-06)
        upper = jnp.dot(at_ref[rows, :], a_ref[:, i * size :], preferred_element_type=jnp.float32)
        lower = jnp.dot(bt_ref[rows, :], a_ref[:, : (i + 1) * size], preferred_element_type=jnp.float32)
        keep = lax.broadcasted_iota(jnp.int32, (size, size), 0) <= lax.broadcasted_iota(jnp.int32, (size, size), 1)
        for j in range(4):
            cols = slice(j * size, (j + 1) * size)
            if j < i:
                part = lower[:, cols]
            elif j > i:
                part = upper[:, (j - i) * size : (j - i + 1) * size]
            else:
                part = jnp.where(keep, upper[:, :size], lower[:, cols])
            stage[rows, cols] = (part * col_gain * row_gain[:, cols]).astype(jnp.bfloat16)
        copies.append(pltpu.make_async_copy(stage.at[rows, :], out_ref.at[0, rows, :], sems.at[i]))
        copies[-1].start()
    for copy in copies:
        copy.wait()


def fold_rows(time_count, tiles, tiles_local):
    fold = np.zeros((2, time_count, tiles_local, time_count, tiles, 2), np.float32)
    for r in range(2):
        for t in range(time_count):
            for u in range(tiles_local):
                fold[r, t, u, t, u, r] = 1.0
            if t:
                fold[r, t, 0, t - 1, tiles_local, r] = 1.0
    return fold.reshape(2 * time_count * tiles_local, -1).astype(ml_dtypes.bfloat16)


def lane_turn():
    turn = np.zeros((4, 4, 32, 4, 4, 32), np.float32)
    for i in range(4):
        for u in range(4):
            for a in range(32):
                turn[i, u, a, u, i, a] = 1.0
    return turn.reshape(512, 512).astype(ml_dtypes.bfloat16)


def body(voltages):
    inp_count = lax.axis_size("inp")
    time_count = lax.axis_size("tm")
    devices = inp_count * time_count
    local_inputs = voltages.shape[0]
    spec_local = voltages.shape[1] // NFFT
    slots = spec_local + 4
    tiles = slots * local_inputs // LANES
    tiles_local = spec_local * local_inputs // LANES
    block = 128
    steps = CHANNELS // block
    sent = pl.pallas_call(
        lambda *refs: front_kernel(spec_local, slots, *refs),
        grid=(steps,),
        in_specs=[
            pl.BlockSpec(voltages.shape, lambda i: (0, 0)),
            pl.BlockSpec((TAPS, NFFT), lambda i: (0, 0)),
            pl.BlockSpec((2 * block, NFFT), lambda i: (i, 0)),
        ],
        out_specs=pl.BlockSpec((block * 2 * tiles, LANES), lambda i: (i, 0)),
        out_shape=jax.ShapeDtypeStruct((CHANNELS * 2 * tiles, LANES), jnp.bfloat16),
        scratch_shapes=[
            pltpu.VMEM((slots * local_inputs, NFFT), jnp.bfloat16),
            pltpu.VMEM((block * 2 * tiles, LANES), jnp.float32),
        ],
        compiler_params=pltpu.CompilerParams(vmem_limit_bytes=24 * 1024 * 1024),
    )(voltages, jnp.asarray(filter_window()), jnp.asarray(phase_rows(block)))
    got = lax.all_to_all(
        sent.reshape(devices, tiles, 2, LANES), ("inp", "tm"), split_axis=0, concat_axis=0, tiled=True
    )
    got = got.reshape(inp_count, time_count * tiles * 2, LANES)
    total_spectra = spec_local * time_count
    inputs = inp_count * local_inputs
    depth = 2 * total_spectra
    vmem = pl.BlockSpec(memory_space=pltpu.VMEM)
    return pl.pallas_call(
        lambda *refs: back_kernel(inputs // LANES, total_spectra, *refs),
        in_specs=[vmem] * 3,
        out_specs=pl.BlockSpec(memory_space=pl.ANY),
        out_shape=jax.ShapeDtypeStruct((1, inputs, inputs), jnp.bfloat16),
        scratch_shapes=[
            pltpu.VMEM((depth, inputs), jnp.bfloat16),
            pltpu.VMEM((inputs, depth), jnp.bfloat16),
            pltpu.VMEM((inputs, depth), jnp.bfloat16),
            pltpu.VMEM((inputs, inputs), jnp.bfloat16),
            pltpu.SemaphoreType.DMA((4,)),
        ],
        compiler_params=pltpu.CompilerParams(vmem_limit_bytes=24 * 1024 * 1024),
    )(got, jnp.asarray(fold_rows(time_count, tiles, tiles_local)), jnp.asarray(lane_turn()))


def solution(mesh):
    in_specs = (P("inp", "tm"),)
    out_specs = P(("inp", "tm"), None, None)
    return jax.shard_map(body, mesh=mesh, in_specs=in_specs, out_specs=out_specs, check_vma=False)
```

```python
import math

import jax
import jax.numpy as jnp
import ml_dtypes
import numpy as np
from jax import lax
from jax.experimental import pallas as pl
from jax.experimental.pallas import tpu as pltpu
from jax.sharding import PartitionSpec as P

NFFT = 2048
CHANNELS = 512
TAPS = 4
LANES = 128


def filter_window():
    sample = np.arange(TAPS * NFFT, dtype=np.float64) + 0.5
    shaped = np.sinc(sample / NFFT - TAPS / 2.0)
    tapered = 0.5 - 0.5 * np.cos(2.0 * math.pi * sample / (TAPS * NFFT))
    return (shaped * tapered).reshape(TAPS, NFFT).astype(np.float32)


def phase_rows(block):
    sample = np.arange(NFFT // 4, dtype=np.int64)
    bin_index = NFFT // 2 - CHANNELS + np.arange(CHANNELS, dtype=np.int64)
    product = (bin_index[:, None] * sample[None, :]) % NFFT
    angle = (product.astype(np.float32) * np.float32(2.0 * math.pi / NFFT)).astype(np.float64)
    paired = np.stack([np.cos(angle), -np.sin(angle)]).astype(np.float32)
    paired = paired.reshape(2, block, 4, NFFT // 4).transpose(2, 0, 1, 3)
    return paired.reshape(2 * CHANNELS, NFFT // 4).astype(ml_dtypes.bfloat16)


def front_kernel(v_hbm, w_hbm, t_hbm, out_hbm, v_ref, w_ref, t_ref, filt, stage, packed, v_sem, w_sem, t_sem, o_sem):
    inputs = v_ref.shape[0]
    spec_local = v_ref.shape[1] // NFFT
    per_tile = LANES // inputs
    tiles = filt.shape[0] // LANES
    block = t_ref.shape[0] // 8
    parts = v_sem.shape[0]
    width = v_ref.shape[1] // parts
    fetch_v = [
        pltpu.make_async_copy(
            v_hbm.at[:, i * width : (i + 1) * width], v_ref.at[:, i * width : (i + 1) * width], v_sem.at[i]
        )
        for i in range(parts)
    ]
    fetch_w = pltpu.make_async_copy(w_hbm, w_ref, w_sem)
    fetch_t = pltpu.make_async_copy(t_hbm, t_ref, t_sem)
    fetch_w.start()
    fetch_v[0].start()
    fetch_v[1].start()
    fetch_t.start()
    fetch_v[2].start()
    fetch_v[3].start()
    fetch_w.wait()

    def filter_tiles(first, last, off):
        weights = [w_ref[k : k + 1, pl.ds(off, LANES)] for k in range(TAPS)]
        slots = range(first * per_tile, last * per_tile)
        need = sorted({j + k - TAPS + 1 for j in slots for k in range(TAPS)} & set(range(spec_local)))
        rows = {
            s: v_ref[:, pl.ds(pl.multiple_of(s * NFFT + off, LANES), LANES)].astype(jnp.float32) for s in need
        }
        for j in slots:
            total = None
            for k in range(TAPS):
                s = j + k - TAPS + 1
                if s in rows:
                    term = weights[k] * rows[s]
                    total = term if total is None else total + term
            if total is None:
                total = jnp.zeros((inputs, LANES), jnp.float32)
            filt[j * inputs : (j + 1) * inputs, pl.ds(off, LANES)] = total.astype(jnp.bfloat16)

    def phases(residue):
        real = t_ref[2 * residue * block : (2 * residue + 1) * block, :]
        imag = t_ref[(2 * residue + 1) * block : (2 * residue + 2) * block, :]
        turns = [(real, imag), (imag, -real), (-real, -imag), (-imag, real)]
        quarters = [turns[(residue * q) % 4] for q in range(4)]
        return jnp.concatenate([jnp.concatenate([part[r] for part in quarters], axis=1) for r in range(2)], axis=0)

    def transform(first, last):
        for residue in range(4):
            acc = lax.dot_general(
                phases(residue),
                filt[first * LANES : last * LANES, :],
                (((1,), (1,)), ((), ())),
                preferred_element_type=jnp.float32,
            )
            for t in range(first, last):
                for r in range(2):
                    stage[pl.ds(residue * 2 * tiles + 2 * t + r, block, stride=8 * tiles), :] = acc[
                        r * block : (r + 1) * block, (t - first) * LANES : (t - first + 1) * LANES
                    ]

    fetch_v[0].wait()
    fetch_v[1].wait()

    @pl.loop(0, NFFT // LANES)
    def _(q):
        filter_tiles(0, 2, pl.multiple_of(q * LANES, LANES))

    fetch_v[2].wait()
    fetch_v[3].wait()
    fetch_t.wait()
    transform(0, 2)
    for q in range(NFFT // LANES):
        filter_tiles(2, 4, q * LANES)
    for q in range(NFFT // LANES):
        filter_tiles(4, tiles, q * LANES)
    transform(2, tiles)
    size = packed.shape[0] // 4
    stores = []
    for i in range(4):
        rows = slice(i * size, (i + 1) * size)
        packed[rows, :] = stage[rows, :].astype(jnp.bfloat16)
        stores.append(pltpu.make_async_copy(packed.at[rows, :], out_hbm.at[rows, :], o_sem.at[i]))
        stores[-1].start()
    for store in stores:
        store.wait()


def back_kernel(groups, total_spectra, x_ref, fold_ref, perm_ref, out_ref, a_ref, at_ref, bt_ref, stage, sems):
    per_group = LANES * 4
    inputs = groups * LANES
    depth = a_ref.shape[0]
    half_sign = jnp.where(lax.broadcasted_iota(jnp.int32, (1, LANES), 1) < LANES // 2, 1.0, -1.0)
    for g in range(groups):
        joined = jnp.concatenate([x_ref[4 * g + i] for i in range(4)], axis=1)
        spectra = jnp.dot(fold_ref[...], joined, preferred_element_type=jnp.float32).astype(jnp.bfloat16)
        turned = jnp.dot(spectra, perm_ref[...], preferred_element_type=jnp.float32).astype(jnp.bfloat16)
        flipped = lax.dot_general(
            perm_ref[...], spectra, (((1,), (1,)), ((), ())), preferred_element_type=jnp.float32
        )
        swapped = pltpu.roll(flipped, LANES // 2, 1) * half_sign
        flipped = flipped.astype(jnp.bfloat16)
        swapped = swapped.astype(jnp.bfloat16)
        for u in range(4):
            rows = slice(u * LANES, (u + 1) * LANES)
            cols = slice(g * LANES, (g + 1) * LANES)
            a_ref[rows, cols] = turned[:, rows]
            at_ref[cols, rows] = flipped[rows, :]
            bt_ref[cols, rows] = swapped[rows, :]
    scale = 1.0 / total_spectra
    wide = a_ref[...].astype(jnp.float32)
    row_gain = lax.rsqrt(jnp.sum(wide * wide, axis=0, keepdims=True) * scale + 1e-06) * scale
    size = inputs // 4
    copies = []
    for i in range(4):
        rows = slice(i * size, (i + 1) * size)
        tall = at_ref[rows, :].astype(jnp.float32)
        col_gain = lax.rsqrt(jnp.sum(tall * tall, axis=1, keepdims=True) * scale + 1e-06)
        upper = jnp.dot(at_ref[rows, :], a_ref[:, i * size :], preferred_element_type=jnp.float32)
        lower = jnp.dot(bt_ref[rows, :], a_ref[:, : (i + 1) * size], preferred_element_type=jnp.float32)
        keep = lax.broadcasted_iota(jnp.int32, (size, size), 0) <= lax.broadcasted_iota(jnp.int32, (size, size), 1)
        for j in range(4):
            cols = slice(j * size, (j + 1) * size)
            if j < i:
                part = lower[:, cols]
            elif j > i:
                part = upper[:, (j - i) * size : (j - i + 1) * size]
            else:
                part = jnp.where(keep, upper[:, :size], lower[:, cols])
            stage[rows, cols] = (part * col_gain * row_gain[:, cols]).astype(jnp.bfloat16)
        copies.append(pltpu.make_async_copy(stage.at[rows, :], out_ref.at[0, rows, :], sems.at[i]))
        copies[-1].start()
    for copy in copies:
        copy.wait()


def fold_rows(time_count, tiles, tiles_local):
    fold = np.zeros((2, time_count, tiles_local, time_count, tiles, 2), np.float32)
    for r in range(2):
        for t in range(time_count):
            for u in range(tiles_local):
                fold[r, t, u, t, u, r] = 1.0
            if t:
                fold[r, t, 0, t - 1, tiles_local, r] = 1.0
    return fold.reshape(2 * time_count * tiles_local, -1).astype(ml_dtypes.bfloat16)


def lane_turn():
    turn = np.zeros((4, 4, 32, 4, 4, 32), np.float32)
    for i in range(4):
        for u in range(4):
            for a in range(32):
                turn[i, u, a, u, i, a] = 1.0
    return turn.reshape(512, 512).astype(ml_dtypes.bfloat16)


def body(voltages):
    inp_count = lax.axis_size("inp")
    time_count = lax.axis_size("tm")
    devices = inp_count * time_count
    local_inputs = voltages.shape[0]
    spec_local = voltages.shape[1] // NFFT
    slots = spec_local + 4
    tiles = slots * local_inputs // LANES
    tiles_local = spec_local * local_inputs // LANES
    block = CHANNELS // 4
    rows = CHANNELS * 2 * tiles
    hbm = pl.BlockSpec(memory_space=pl.ANY)
    sent = pl.pallas_call(
        front_kernel,
        in_specs=[hbm] * 3,
        out_specs=hbm,
        out_shape=jax.ShapeDtypeStruct((rows, LANES), jnp.bfloat16),
        scratch_shapes=[
            pltpu.VMEM(voltages.shape, jnp.bfloat16),
            pltpu.VMEM((TAPS, NFFT), jnp.float32),
            pltpu.VMEM((2 * CHANNELS, NFFT // 4), jnp.bfloat16),
            pltpu.VMEM((slots * local_inputs, NFFT), jnp.bfloat16),
            pltpu.VMEM((rows, LANES), jnp.float32),
            pltpu.VMEM((rows, LANES), jnp.bfloat16),
            pltpu.SemaphoreType.DMA((4,)),
            pltpu.SemaphoreType.DMA,
            pltpu.SemaphoreType.DMA,
            pltpu.SemaphoreType.DMA((4,)),
        ],
        compiler_params=pltpu.CompilerParams(vmem_limit_bytes=60 * 1024 * 1024),
    )(voltages, jnp.asarray(filter_window()), jnp.asarray(phase_rows(block)))
    got = lax.all_to_all(
        sent.reshape(devices, tiles, 2, LANES), ("inp", "tm"), split_axis=0, concat_axis=0, tiled=True
    )
    got = got.reshape(inp_count, time_count * tiles * 2, LANES)
    total_spectra = spec_local * time_count
    inputs = inp_count * local_inputs
    depth = 2 * total_spectra
    vmem = pl.BlockSpec(memory_space=pltpu.VMEM)
    return pl.pallas_call(
        lambda *refs: back_kernel(inputs // LANES, total_spectra, *refs),
        in_specs=[vmem] * 3,
        out_specs=pl.BlockSpec(memory_space=pl.ANY),
        out_shape=jax.ShapeDtypeStruct((1, inputs, inputs), jnp.bfloat16),
        scratch_shapes=[
            pltpu.VMEM((depth, inputs), jnp.bfloat16),
            pltpu.VMEM((inputs, depth), jnp.bfloat16),
            pltpu.VMEM((inputs, depth), jnp.bfloat16),
            pltpu.VMEM((inputs, inputs), jnp.bfloat16),
            pltpu.SemaphoreType.DMA((4,)),
        ],
        compiler_params=pltpu.CompilerParams(vmem_limit_bytes=24 * 1024 * 1024),
    )(got, jnp.asarray(fold_rows(time_count, tiles, tiles_local)), jnp.asarray(lane_turn()))


def solution(mesh):
    in_specs = (P("inp", "tm"),)
    out_specs = P(("inp", "tm"), None, None)
    return jax.shard_map(body, mesh=mesh, in_specs=in_specs, out_specs=out_specs, check_vma=False)
```

```python
import math

import jax
import jax.numpy as jnp
import ml_dtypes
import numpy as np
from jax import lax
from jax.experimental import pallas as pl
from jax.experimental.pallas import tpu as pltpu
from jax.sharding import PartitionSpec as P

NFFT = 2048
CHANNELS = 512
TAPS = 4
LANES = 128


def filter_window():
    sample = np.arange(TAPS * NFFT, dtype=np.float64) + 0.5
    shaped = np.sinc(sample / NFFT - TAPS / 2.0)
    tapered = 0.5 - 0.5 * np.cos(2.0 * math.pi * sample / (TAPS * NFFT))
    return (shaped * tapered).reshape(TAPS, NFFT).astype(np.float32)


def phase_rows(block):
    sample = np.arange(NFFT // 4, dtype=np.int64)
    bin_index = NFFT // 2 - CHANNELS + np.arange(CHANNELS, dtype=np.int64)
    product = (bin_index[:, None] * sample[None, :]) % NFFT
    angle = (product.astype(np.float32) * np.float32(2.0 * math.pi / NFFT)).astype(np.float64)
    paired = np.stack([np.cos(angle), -np.sin(angle)]).astype(np.float32)
    paired = paired.reshape(2, block, 4, NFFT // 4).transpose(2, 0, 1, 3)[:, :, ::-1]
    return paired.reshape(2 * CHANNELS, NFFT // 4).astype(ml_dtypes.bfloat16)


def front_kernel(v_hbm, w_hbm, t_hbm, out_hbm, v_ref, w_ref, t_ref, filt, stage, packed, v_sem, w_sem, t_sem, o_sem):
    inputs = v_ref.shape[0]
    spec_local = v_ref.shape[1] // NFFT
    per_tile = LANES // inputs
    tiles = filt.shape[0] // LANES
    block = t_ref.shape[0] // 8
    parts = v_sem.shape[0]
    width = v_ref.shape[1] // parts
    fetch_v = [
        pltpu.make_async_copy(
            v_hbm.at[:, i * width : (i + 1) * width], v_ref.at[:, i * width : (i + 1) * width], v_sem.at[i]
        )
        for i in range(parts)
    ]
    fetch_w = pltpu.make_async_copy(w_hbm, w_ref, w_sem)
    fetch_t = pltpu.make_async_copy(t_hbm, t_ref, t_sem)
    fetch_w.start()
    fetch_v[0].start()
    fetch_v[1].start()
    fetch_t.start()
    fetch_v[2].start()
    fetch_v[3].start()
    fetch_w.wait()

    def filter_tiles(first, last, off):
        weights = [w_ref[k : k + 1, pl.ds(off, LANES)] for k in range(TAPS)]
        slots = range(first * per_tile, last * per_tile)
        need = sorted({j + k - TAPS + 1 for j in slots for k in range(TAPS)} & set(range(spec_local)))
        rows = {
            s: v_ref[:, pl.ds(pl.multiple_of(s * NFFT + off, LANES), LANES)].astype(jnp.float32) for s in need
        }
        for j in slots:
            total = None
            for k in range(TAPS):
                s = j + k - TAPS + 1
                if s in rows:
                    term = weights[k] * rows[s]
                    total = term if total is None else total + term
            if total is None:
                total = jnp.zeros((inputs, LANES), jnp.float32)
            filt[j * inputs : (j + 1) * inputs, pl.ds(off, LANES)] = total.astype(jnp.bfloat16)

    def phases(residue):
        real = t_ref[2 * residue * block : (2 * residue + 1) * block, :]
        imag = t_ref[(2 * residue + 1) * block : (2 * residue + 2) * block, :]
        turns = [(real, imag), (imag, -real), (-real, -imag), (-imag, real)]
        quarters = [turns[(residue * q) % 4] for q in range(4)]
        return jnp.concatenate([jnp.concatenate([part[r] for part in quarters], axis=1) for r in range(2)], axis=0)

    def transform(first, last):
        for residue in range(4):
            acc = lax.dot_general(
                phases(residue),
                filt[first * LANES : last * LANES, :],
                (((1,), (1,)), ((), ())),
                preferred_element_type=jnp.float32,
            )
            for t in range(first, last):
                for r in range(2):
                    stage[pl.ds((3 - residue) * 2 * tiles + 2 * t + r, block, stride=8 * tiles), :] = acc[
                        r * block : (r + 1) * block, (t - first) * LANES : (t - first + 1) * LANES
                    ]

    fetch_v[0].wait()
    fetch_v[1].wait()

    @pl.loop(0, NFFT // LANES)
    def _(q):
        filter_tiles(0, 2, pl.multiple_of(q * LANES, LANES))

    fetch_v[2].wait()
    fetch_v[3].wait()
    fetch_t.wait()
    transform(0, 2)
    for q in range(NFFT // LANES):
        filter_tiles(2, 4, q * LANES)
    for q in range(NFFT // LANES):
        filter_tiles(4, tiles, q * LANES)
    transform(2, tiles)
    size = packed.shape[0] // 4
    stores = []
    for i in range(4):
        rows = slice(i * size, (i + 1) * size)
        packed[rows, :] = stage[rows, :].astype(jnp.bfloat16)
        stores.append(pltpu.make_async_copy(packed.at[rows, :], out_hbm.at[rows, :], o_sem.at[i]))
        stores[-1].start()
    for store in stores:
        store.wait()


def back_kernel(groups, total_spectra, x_ref, fold_ref, perm_ref, out_ref, a_ref, at_ref, bt_ref, stage, sems):
    per_group = LANES * 4
    inputs = groups * LANES
    depth = a_ref.shape[0]
    half_sign = jnp.where(lax.broadcasted_iota(jnp.int32, (1, LANES), 1) < LANES // 2, 1.0, -1.0)
    for g in range(groups):
        joined = jnp.concatenate([x_ref[4 * groups - 1 - 4 * g - i] for i in range(4)], axis=1)
        spectra = jnp.dot(fold_ref[...], joined, preferred_element_type=jnp.float32).astype(jnp.bfloat16)
        turned = jnp.dot(spectra, perm_ref[...], preferred_element_type=jnp.float32).astype(jnp.bfloat16)
        flipped = lax.dot_general(
            perm_ref[...], spectra, (((1,), (1,)), ((), ())), preferred_element_type=jnp.float32
        )
        swapped = pltpu.roll(flipped, LANES // 2, 1) * half_sign
        flipped = flipped.astype(jnp.bfloat16)
        swapped = swapped.astype(jnp.bfloat16)
        for u in range(4):
            rows = slice(u * LANES, (u + 1) * LANES)
            cols = slice(g * LANES, (g + 1) * LANES)
            a_ref[rows, cols] = turned[:, rows]
            at_ref[cols, rows] = flipped[rows, :]
            bt_ref[cols, rows] = swapped[rows, :]
    scale = 1.0 / total_spectra
    wide = a_ref[...].astype(jnp.float32)
    row_gain = lax.rsqrt(jnp.sum(wide * wide, axis=0, keepdims=True) * scale + 1e-06) * scale
    size = inputs // 4
    copies = []
    for i in range(4):
        rows = slice(i * size, (i + 1) * size)
        tall = at_ref[rows, :].astype(jnp.float32)
        col_gain = lax.rsqrt(jnp.sum(tall * tall, axis=1, keepdims=True) * scale + 1e-06)
        upper = jnp.dot(at_ref[rows, :], a_ref[:, i * size :], preferred_element_type=jnp.float32)
        lower = jnp.dot(bt_ref[rows, :], a_ref[:, : (i + 1) * size], preferred_element_type=jnp.float32)
        keep = lax.broadcasted_iota(jnp.int32, (size, size), 0) <= lax.broadcasted_iota(jnp.int32, (size, size), 1)
        for j in range(4):
            cols = slice(j * size, (j + 1) * size)
            if j < i:
                part = lower[:, cols]
            elif j > i:
                part = upper[:, (j - i) * size : (j - i + 1) * size]
            else:
                part = jnp.where(keep, upper[:, :size], lower[:, cols])
            stage[rows, cols] = (part * col_gain * row_gain[:, cols]).astype(jnp.bfloat16)
        copies.append(pltpu.make_async_copy(stage.at[rows, :], out_ref.at[0, rows, :], sems.at[i]))
        copies[-1].start()
    for copy in copies:
        copy.wait()


def fold_rows(time_count, tiles, tiles_local):
    fold = np.zeros((2, time_count, tiles_local, time_count, tiles, 2), np.float32)
    for r in range(2):
        for t in range(time_count):
            for u in range(tiles_local):
                fold[r, t, u, t, u, r] = 1.0
            if t:
                fold[r, t, 0, t - 1, tiles_local, r] = 1.0
    return fold[:, :, :, ::-1].reshape(2 * time_count * tiles_local, -1).astype(ml_dtypes.bfloat16)


def lane_turn():
    turn = np.zeros((4, 4, 32, 4, 4, 32), np.float32)
    for i in range(4):
        for u in range(4):
            for a in range(32):
                turn[i, u, a, u, i, a] = 1.0
    return turn.reshape(512, 512).astype(ml_dtypes.bfloat16)


def body(voltages):
    inp_count = lax.axis_size("inp")
    time_count = lax.axis_size("tm")
    devices = inp_count * time_count
    local_inputs = voltages.shape[0]
    spec_local = voltages.shape[1] // NFFT
    slots = spec_local + 4
    tiles = slots * local_inputs // LANES
    tiles_local = spec_local * local_inputs // LANES
    block = CHANNELS // 4
    rows = CHANNELS * 2 * tiles
    hbm = pl.BlockSpec(memory_space=pl.ANY)
    sent = pl.pallas_call(
        front_kernel,
        in_specs=[hbm] * 3,
        out_specs=hbm,
        out_shape=jax.ShapeDtypeStruct((rows, LANES), jnp.bfloat16),
        scratch_shapes=[
            pltpu.VMEM(voltages.shape, jnp.bfloat16),
            pltpu.VMEM((TAPS, NFFT), jnp.float32),
            pltpu.VMEM((2 * CHANNELS, NFFT // 4), jnp.bfloat16),
            pltpu.VMEM((slots * local_inputs, NFFT), jnp.bfloat16),
            pltpu.VMEM((rows, LANES), jnp.float32),
            pltpu.VMEM((rows, LANES), jnp.bfloat16),
            pltpu.SemaphoreType.DMA((4,)),
            pltpu.SemaphoreType.DMA,
            pltpu.SemaphoreType.DMA,
            pltpu.SemaphoreType.DMA((4,)),
        ],
        compiler_params=pltpu.CompilerParams(vmem_limit_bytes=60 * 1024 * 1024),
    )(voltages, jnp.asarray(filter_window()), jnp.asarray(phase_rows(block)))
    got = lax.all_to_all(
        sent.reshape(devices, tiles, 2, LANES),
        ("inp", "tm"),
        split_axis=0,
        concat_axis=0,
        axis_index_groups=[list(reversed(range(devices)))],
        tiled=True,
    )
    got = got.reshape(inp_count, time_count * tiles * 2, LANES)
    total_spectra = spec_local * time_count
    inputs = inp_count * local_inputs
    depth = 2 * total_spectra
    vmem = pl.BlockSpec(memory_space=pltpu.VMEM)
    return pl.pallas_call(
        lambda *refs: back_kernel(inputs // LANES, total_spectra, *refs),
        in_specs=[vmem] * 3,
        out_specs=pl.BlockSpec(memory_space=pl.ANY),
        out_shape=jax.ShapeDtypeStruct((1, inputs, inputs), jnp.bfloat16),
        scratch_shapes=[
            pltpu.VMEM((depth, inputs), jnp.bfloat16),
            pltpu.VMEM((inputs, depth), jnp.bfloat16),
            pltpu.VMEM((inputs, depth), jnp.bfloat16),
            pltpu.VMEM((inputs, inputs), jnp.bfloat16),
            pltpu.SemaphoreType.DMA((4,)),
        ],
        compiler_params=pltpu.CompilerParams(vmem_limit_bytes=24 * 1024 * 1024),
    )(got, jnp.asarray(fold_rows(time_count, tiles, tiles_local)), jnp.asarray(lane_turn()))


def solution(mesh):
    in_specs = (P("inp", "tm"),)
    out_specs = P(("inp", "tm"), None, None)
    return jax.shard_map(body, mesh=mesh, in_specs=in_specs, out_specs=out_specs, check_vma=False)
```

```python
import math

import jax
import jax.numpy as jnp
import ml_dtypes
import numpy as np
from jax import lax
from jax.experimental import pallas as pl
from jax.experimental.pallas import tpu as pltpu
from jax.sharding import PartitionSpec as P

NFFT = 2048
CHANNELS = 512
TAPS = 4
LANES = 128


def filter_window():
    sample = np.arange(TAPS * NFFT, dtype=np.float64) + 0.5
    shaped = np.sinc(sample / NFFT - TAPS / 2.0)
    tapered = 0.5 - 0.5 * np.cos(2.0 * math.pi * sample / (TAPS * NFFT))
    return (shaped * tapered).reshape(TAPS, NFFT).astype(np.float32)


def phase_rows(block):
    sample = np.arange(NFFT // 4, dtype=np.int64)
    bin_index = NFFT // 2 - CHANNELS + np.arange(CHANNELS, dtype=np.int64)
    product = (bin_index[:, None] * sample[None, :]) % NFFT
    angle = (product.astype(np.float32) * np.float32(2.0 * math.pi / NFFT)).astype(np.float64)
    paired = np.stack([np.cos(angle), -np.sin(angle)]).astype(np.float32)
    paired = paired.reshape(2, block, 4, NFFT // 4).transpose(2, 0, 1, 3)[:, :, ::-1]
    return paired.reshape(2 * CHANNELS, NFFT // 4).astype(ml_dtypes.bfloat16)


def front_kernel(v_hbm, w_hbm, t_hbm, out_hbm, v_ref, w_ref, t_ref, filt, stage, packed, v_sem, w_sem, t_sem, o_sem):
    inputs = v_ref.shape[0]
    spec_local = v_ref.shape[1] // NFFT
    per_tile = LANES // inputs
    tiles = filt.shape[0] // LANES
    block = t_ref.shape[0] // 8
    parts = v_sem.shape[0]
    width = v_ref.shape[1] // parts
    fetch_v = [
        pltpu.make_async_copy(
            v_hbm.at[:, i * width : (i + 1) * width], v_ref.at[:, i * width : (i + 1) * width], v_sem.at[i]
        )
        for i in range(parts)
    ]
    fetch_w = pltpu.make_async_copy(w_hbm, w_ref, w_sem)
    fetch_t = pltpu.make_async_copy(t_hbm, t_ref, t_sem)
    fetch_w.start()
    fetch_v[0].start()
    fetch_v[1].start()
    fetch_t.start()
    fetch_v[2].start()
    fetch_v[3].start()
    fetch_w.wait()

    def filter_tiles(first, last, off):
        weights = [w_ref[k : k + 1, pl.ds(off, LANES)] for k in range(TAPS)]
        slots = range(first * per_tile, last * per_tile)
        need = sorted({j + k - TAPS + 1 for j in slots for k in range(TAPS)} & set(range(spec_local)))
        rows = {
            s: v_ref[:, pl.ds(pl.multiple_of(s * NFFT + off, LANES), LANES)].astype(jnp.float32) for s in need
        }
        for j in slots:
            total = None
            for k in range(TAPS):
                s = j + k - TAPS + 1
                if s in rows:
                    term = weights[k] * rows[s]
                    total = term if total is None else total + term
            if total is None:
                total = jnp.zeros((inputs, LANES), jnp.float32)
            filt[j * inputs : (j + 1) * inputs, pl.ds(off, LANES)] = total.astype(jnp.bfloat16)

    def phases(residue):
        real = t_ref[2 * residue * block : (2 * residue + 1) * block, :]
        imag = t_ref[(2 * residue + 1) * block : (2 * residue + 2) * block, :]
        turns = [(real, imag), (imag, -real), (-real, -imag), (-imag, real)]
        quarters = [turns[(residue * q) % 4] for q in range(4)]
        return jnp.concatenate([jnp.concatenate([part[r] for part in quarters], axis=1) for r in range(2)], axis=0)

    def transform(first, last):
        for residue in range(4):
            acc = lax.dot_general(
                phases(residue),
                filt[first * LANES : last * LANES, :],
                (((1,), (1,)), ((), ())),
                preferred_element_type=jnp.float32,
            )
            for t in range(first, last):
                for r in range(2):
                    stage[pl.ds((3 - residue) * 2 * tiles + 2 * t + r, block, stride=8 * tiles), :] = acc[
                        r * block : (r + 1) * block, (t - first) * LANES : (t - first + 1) * LANES
                    ]

    fetch_v[0].wait()
    fetch_v[1].wait()

    @pl.loop(0, NFFT // LANES)
    def _(q):
        filter_tiles(0, 2, pl.multiple_of(q * LANES, LANES))

    fetch_v[2].wait()
    fetch_v[3].wait()
    fetch_t.wait()
    transform(0, 2)
    for q in range(NFFT // LANES):
        filter_tiles(2, 4, q * LANES)
    for q in range(NFFT // LANES):
        filter_tiles(4, tiles, q * LANES)
    transform(2, tiles)
    size = packed.shape[0] // 4
    stores = []
    for i in range(4):
        rows = slice(i * size, (i + 1) * size)
        packed[rows, :] = stage[rows, :].astype(jnp.bfloat16)
        stores.append(pltpu.make_async_copy(packed.at[rows, :], out_hbm.at[rows, :], o_sem.at[i]))
        stores[-1].start()
    for store in stores:
        store.wait()


def back_kernel(groups, total_spectra, x_ref, fold_ref, perm_ref, out_ref, a_ref, at_ref, bt_ref, stage, sems):
    inputs = groups * LANES
    half = LANES // 2
    for h in range(groups // 2):
        folded = []
        for g in (2 * h, 2 * h + 1):
            joined = jnp.concatenate([x_ref[4 * groups - 1 - 4 * g - i] for i in range(4)], axis=1)
            spectra = jnp.dot(fold_ref[...], joined, preferred_element_type=jnp.float32)
            folded.append(spectra.astype(jnp.bfloat16))
        turned = jnp.dot(
            jnp.concatenate(folded, axis=0), perm_ref[...], preferred_element_type=jnp.float32
        ).astype(jnp.bfloat16)
        for k in range(2):
            cols = slice((2 * h + k) * LANES, (2 * h + k + 1) * LANES)
            for u in range(4):
                rows = slice(u * LANES, (u + 1) * LANES)
                part = turned[k * LANES : (k + 1) * LANES, rows]
                a_ref[rows, cols] = part
                at_ref[cols, rows] = part.T
                bt_ref[cols, rows] = jnp.concatenate([part[half:], -part[:half]], axis=0).T
    scale = 1.0 / total_spectra
    wide = a_ref[...].astype(jnp.float32)
    row_gain = lax.rsqrt(jnp.sum(wide * wide, axis=0, keepdims=True) * scale + 1e-06) * scale
    size = inputs // 4
    copies = []
    for i in range(4):
        rows = slice(i * size, (i + 1) * size)
        tall = at_ref[rows, :].astype(jnp.float32)
        col_gain = lax.rsqrt(jnp.sum(tall * tall, axis=1, keepdims=True) * scale + 1e-06)
        upper = jnp.dot(at_ref[rows, :], a_ref[:, i * size :], preferred_element_type=jnp.float32)
        lower = jnp.dot(bt_ref[rows, :], a_ref[:, : (i + 1) * size], preferred_element_type=jnp.float32)
        keep = lax.broadcasted_iota(jnp.int32, (size, size), 0) <= lax.broadcasted_iota(jnp.int32, (size, size), 1)
        for j in range(4):
            cols = slice(j * size, (j + 1) * size)
            if j < i:
                part = lower[:, cols]
            elif j > i:
                part = upper[:, (j - i) * size : (j - i + 1) * size]
            else:
                part = jnp.where(keep, upper[:, :size], lower[:, cols])
            stage[rows, cols] = (part * col_gain * row_gain[:, cols]).astype(jnp.bfloat16)
        copies.append(pltpu.make_async_copy(stage.at[rows, :], out_ref.at[0, rows, :], sems.at[i]))
        copies[-1].start()
    for copy in copies:
        copy.wait()


def fold_rows(time_count, tiles, tiles_local):
    fold = np.zeros((2, time_count, tiles_local, time_count, tiles, 2), np.float32)
    for r in range(2):
        for t in range(time_count):
            for u in range(tiles_local):
                fold[r, t, u, t, u, r] = 1.0
            if t:
                fold[r, t, 0, t - 1, tiles_local, r] = 1.0
    return fold[:, :, :, ::-1].reshape(2 * time_count * tiles_local, -1).astype(ml_dtypes.bfloat16)


def lane_turn():
    turn = np.zeros((4, 4, 32, 4, 4, 32), np.float32)
    for i in range(4):
        for u in range(4):
            for a in range(32):
                turn[i, u, a, u, i, a] = 1.0
    return turn.reshape(512, 512).astype(ml_dtypes.bfloat16)


def body(voltages):
    inp_count = lax.axis_size("inp")
    time_count = lax.axis_size("tm")
    devices = inp_count * time_count
    local_inputs = voltages.shape[0]
    spec_local = voltages.shape[1] // NFFT
    slots = spec_local + 4
    tiles = slots * local_inputs // LANES
    tiles_local = spec_local * local_inputs // LANES
    block = CHANNELS // 4
    rows = CHANNELS * 2 * tiles
    hbm = pl.BlockSpec(memory_space=pl.ANY)
    sent = pl.pallas_call(
        front_kernel,
        in_specs=[hbm] * 3,
        out_specs=hbm,
        out_shape=jax.ShapeDtypeStruct((rows, LANES), jnp.bfloat16),
        scratch_shapes=[
            pltpu.VMEM(voltages.shape, jnp.bfloat16),
            pltpu.VMEM((TAPS, NFFT), jnp.float32),
            pltpu.VMEM((2 * CHANNELS, NFFT // 4), jnp.bfloat16),
            pltpu.VMEM((slots * local_inputs, NFFT), jnp.bfloat16),
            pltpu.VMEM((rows, LANES), jnp.float32),
            pltpu.VMEM((rows, LANES), jnp.bfloat16),
            pltpu.SemaphoreType.DMA((4,)),
            pltpu.SemaphoreType.DMA,
            pltpu.SemaphoreType.DMA,
            pltpu.SemaphoreType.DMA((4,)),
        ],
        compiler_params=pltpu.CompilerParams(vmem_limit_bytes=60 * 1024 * 1024),
    )(voltages, jnp.asarray(filter_window()), jnp.asarray(phase_rows(block)))
    got = lax.all_to_all(
        sent.reshape(devices, tiles, 2, LANES),
        ("inp", "tm"),
        split_axis=0,
        concat_axis=0,
        axis_index_groups=[list(reversed(range(devices)))],
        tiled=True,
    )
    got = got.reshape(inp_count, time_count * tiles * 2, LANES)
    total_spectra = spec_local * time_count
    inputs = inp_count * local_inputs
    depth = 2 * total_spectra
    vmem = pl.BlockSpec(memory_space=pltpu.VMEM)
    return pl.pallas_call(
        lambda *refs: back_kernel(inputs // LANES, total_spectra, *refs),
        in_specs=[vmem] * 3,
        out_specs=pl.BlockSpec(memory_space=pl.ANY),
        out_shape=jax.ShapeDtypeStruct((1, inputs, inputs), jnp.bfloat16),
        scratch_shapes=[
            pltpu.VMEM((depth, inputs), jnp.bfloat16),
            pltpu.VMEM((inputs, depth), jnp.bfloat16),
            pltpu.VMEM((inputs, depth), jnp.bfloat16),
            pltpu.VMEM((inputs, inputs), jnp.bfloat16),
            pltpu.SemaphoreType.DMA((4,)),
        ],
        compiler_params=pltpu.CompilerParams(vmem_limit_bytes=24 * 1024 * 1024),
    )(got, jnp.asarray(fold_rows(time_count, tiles, tiles_local)), jnp.asarray(lane_turn()))


def solution(mesh):
    in_specs = (P("inp", "tm"),)
    out_specs = P(("inp", "tm"), None, None)
    return jax.shard_map(body, mesh=mesh, in_specs=in_specs, out_specs=out_specs, check_vma=False)
```

```python
import math

import jax
import jax.numpy as jnp
import ml_dtypes
import numpy as np
from jax import lax
from jax.experimental import pallas as pl
from jax.experimental.pallas import tpu as pltpu
from jax.sharding import PartitionSpec as P

NFFT = 2048
CHANNELS = 512
TAPS = 4
LANES = 128
WINDOW_ROWS = 512
TABLE_ROWS = 2048


def filter_window():
    sample = np.arange(TAPS * NFFT, dtype=np.float64) + 0.5
    shaped = np.sinc(sample / NFFT - TAPS / 2.0)
    tapered = 0.5 - 0.5 * np.cos(2.0 * math.pi * sample / (TAPS * NFFT))
    window = np.zeros((WINDOW_ROWS, NFFT), np.float32)
    window[:TAPS] = (shaped * tapered).reshape(TAPS, NFFT)
    return window


def phase_rows(block):
    sample = np.arange(NFFT // 4, dtype=np.int64)
    bin_index = NFFT // 2 - CHANNELS + np.arange(CHANNELS, dtype=np.int64)
    product = (bin_index[:, None] * sample[None, :]) % NFFT
    angle = (product.astype(np.float32) * np.float32(2.0 * math.pi / NFFT)).astype(np.float64)
    paired = np.stack([np.cos(angle), -np.sin(angle)]).astype(np.float32)
    paired = paired.reshape(2, block, 4, NFFT // 4).transpose(2, 0, 1, 3)[:, :, ::-1]
    table = np.zeros((TABLE_ROWS, NFFT // 4), ml_dtypes.bfloat16)
    table[: 2 * CHANNELS] = paired.reshape(2 * CHANNELS, NFFT // 4).astype(ml_dtypes.bfloat16)
    return table


def front_kernel(v_hbm, w_hbm, t_hbm, out_ref, v_ref, w_ref, t_ref, filt, stage, v_sem, w_sem, t_sem):
    inputs = v_ref.shape[0]
    spec_local = v_ref.shape[1] // NFFT
    per_tile = LANES // inputs
    tiles = filt.shape[0] // LANES
    block = t_ref.shape[0] // 8
    parts = v_sem.shape[0]
    width = v_ref.shape[1] // parts
    fetch_v = [
        pltpu.make_async_copy(
            v_hbm.at[:, i * width : (i + 1) * width], v_ref.at[:, i * width : (i + 1) * width], v_sem.at[i]
        )
        for i in range(parts)
    ]
    fetch_w = pltpu.make_async_copy(w_hbm.at[: w_ref.shape[0]], w_ref, w_sem)
    fetch_t = pltpu.make_async_copy(t_hbm.at[: t_ref.shape[0]], t_ref, t_sem)
    fetch_w.start()
    fetch_v[0].start()
    fetch_v[1].start()
    fetch_t.start()
    fetch_v[2].start()
    fetch_v[3].start()
    fetch_w.wait()

    def filter_tiles(first, last, off):
        weights = [w_ref[k : k + 1, pl.ds(off, LANES)] for k in range(TAPS)]
        slots = range(first * per_tile, last * per_tile)
        need = sorted({j + k - TAPS + 1 for j in slots for k in range(TAPS)} & set(range(spec_local)))
        rows = {
            s: v_ref[:, pl.ds(pl.multiple_of(s * NFFT + off, LANES), LANES)].astype(jnp.float32) for s in need
        }
        for j in slots:
            total = None
            for k in range(TAPS):
                s = j + k - TAPS + 1
                if s in rows:
                    term = weights[k] * rows[s]
                    total = term if total is None else total + term
            if total is None:
                total = jnp.zeros((inputs, LANES), jnp.float32)
            filt[j * inputs : (j + 1) * inputs, pl.ds(off, LANES)] = total.astype(jnp.bfloat16)

    def phases(residue):
        real = t_ref[2 * residue * block : (2 * residue + 1) * block, :]
        imag = t_ref[(2 * residue + 1) * block : (2 * residue + 2) * block, :]
        turns = [(real, imag), (imag, -real), (-real, -imag), (-imag, real)]
        quarters = [turns[(residue * q) % 4] for q in range(4)]
        return jnp.concatenate([jnp.concatenate([part[r] for part in quarters], axis=1) for r in range(2)], axis=0)

    def transform(first, last):
        for residue in range(4):
            acc = lax.dot_general(
                phases(residue),
                filt[first * LANES : last * LANES, :],
                (((1,), (1,)), ((), ())),
                preferred_element_type=jnp.float32,
            )
            for t in range(first, last):
                for r in range(2):
                    stage[pl.ds((3 - residue) * 2 * tiles + 2 * t + r, block, stride=8 * tiles), :] = acc[
                        r * block : (r + 1) * block, (t - first) * LANES : (t - first + 1) * LANES
                    ]

    fetch_v[0].wait()
    fetch_v[1].wait()

    @pl.loop(0, NFFT // LANES)
    def _(q):
        filter_tiles(0, 2, pl.multiple_of(q * LANES, LANES))

    fetch_v[2].wait()
    fetch_v[3].wait()
    fetch_t.wait()
    transform(0, 2)
    for q in range(NFFT // LANES):
        filter_tiles(2, 4, q * LANES)
    for q in range(NFFT // LANES):
        filter_tiles(4, tiles, q * LANES)
    transform(2, tiles)
    out_ref[...] = stage[...].astype(jnp.bfloat16)


def back_kernel(groups, total_spectra, x_ref, fold_ref, perm_ref, out_ref, a_ref, at_ref, bt_ref, stage, sems):
    inputs = groups * LANES
    half = LANES // 2
    for h in range(groups // 2):
        folded = []
        for g in (2 * h, 2 * h + 1):
            joined = jnp.concatenate([x_ref[4 * groups - 1 - 4 * g - i] for i in range(4)], axis=1)
            spectra = jnp.dot(fold_ref[...], joined, preferred_element_type=jnp.float32)
            folded.append(spectra.astype(jnp.bfloat16))
        turned = jnp.dot(
            jnp.concatenate(folded, axis=0), perm_ref[...], preferred_element_type=jnp.float32
        ).astype(jnp.bfloat16)
        for k in range(2):
            cols = slice((2 * h + k) * LANES, (2 * h + k + 1) * LANES)
            for u in range(4):
                rows = slice(u * LANES, (u + 1) * LANES)
                part = turned[k * LANES : (k + 1) * LANES, rows]
                a_ref[rows, cols] = part
                at_ref[cols, rows] = part.T
                bt_ref[cols, rows] = jnp.concatenate([part[half:], -part[:half]], axis=0).T
    scale = 1.0 / total_spectra
    wide = a_ref[...].astype(jnp.float32)
    row_gain = lax.rsqrt(jnp.sum(wide * wide, axis=0, keepdims=True) * scale + 1e-06) * scale
    size = inputs // 4
    copies = []
    for i in range(4):
        rows = slice(i * size, (i + 1) * size)
        tall = at_ref[rows, :].astype(jnp.float32)
        col_gain = lax.rsqrt(jnp.sum(tall * tall, axis=1, keepdims=True) * scale + 1e-06)
        upper = jnp.dot(at_ref[rows, :], a_ref[:, i * size :], preferred_element_type=jnp.float32)
        lower = jnp.dot(bt_ref[rows, :], a_ref[:, : (i + 1) * size], preferred_element_type=jnp.float32)
        keep = lax.broadcasted_iota(jnp.int32, (size, size), 0) <= lax.broadcasted_iota(jnp.int32, (size, size), 1)
        for j in range(4):
            cols = slice(j * size, (j + 1) * size)
            if j < i:
                part = lower[:, cols]
            elif j > i:
                part = upper[:, (j - i) * size : (j - i + 1) * size]
            else:
                part = jnp.where(keep, upper[:, :size], lower[:, cols])
            stage[rows, cols] = (part * col_gain * row_gain[:, cols]).astype(jnp.bfloat16)
        copies.append(pltpu.make_async_copy(stage.at[rows, :], out_ref.at[0, rows, :], sems.at[i]))
        copies[-1].start()
    for copy in copies:
        copy.wait()


def fold_rows(time_count, tiles, tiles_local):
    fold = np.zeros((2, time_count, tiles_local, time_count, tiles, 2), np.float32)
    for r in range(2):
        for t in range(time_count):
            for u in range(tiles_local):
                fold[r, t, u, t, u, r] = 1.0
            if t:
                fold[r, t, 0, t - 1, tiles_local, r] = 1.0
    return fold[:, :, :, ::-1].reshape(2 * time_count * tiles_local, -1).astype(ml_dtypes.bfloat16)


def lane_turn():
    turn = np.zeros((4, 4, 32, 4, 4, 32), np.float32)
    for i in range(4):
        for u in range(4):
            for a in range(32):
                turn[i, u, a, u, i, a] = 1.0
    return turn.reshape(512, 512).astype(ml_dtypes.bfloat16)


def body(voltages):
    inp_count = lax.axis_size("inp")
    time_count = lax.axis_size("tm")
    devices = inp_count * time_count
    local_inputs = voltages.shape[0]
    spec_local = voltages.shape[1] // NFFT
    slots = spec_local + 4
    tiles = slots * local_inputs // LANES
    tiles_local = spec_local * local_inputs // LANES
    block = CHANNELS // 4
    rows = CHANNELS * 2 * tiles
    hbm = pl.BlockSpec(memory_space=pl.ANY)
    sent = pl.pallas_call(
        front_kernel,
        in_specs=[hbm] * 3,
        out_specs=pl.BlockSpec(memory_space=pltpu.VMEM),
        out_shape=jax.ShapeDtypeStruct((rows, LANES), jnp.bfloat16),
        scratch_shapes=[
            pltpu.VMEM(voltages.shape, jnp.bfloat16),
            pltpu.VMEM((8, NFFT), jnp.float32),
            pltpu.VMEM((2 * CHANNELS, NFFT // 4), jnp.bfloat16),
            pltpu.VMEM((slots * local_inputs, NFFT), jnp.bfloat16),
            pltpu.VMEM((rows, LANES), jnp.float32),
            pltpu.SemaphoreType.DMA((4,)),
            pltpu.SemaphoreType.DMA,
            pltpu.SemaphoreType.DMA,
        ],
        compiler_params=pltpu.CompilerParams(vmem_limit_bytes=51 * 1024 * 1024),
    )(voltages, jnp.asarray(filter_window()), jnp.asarray(phase_rows(block)))
    got = lax.all_to_all(
        sent.reshape(devices, tiles, 2, LANES),
        ("inp", "tm"),
        split_axis=0,
        concat_axis=0,
        axis_index_groups=[list(reversed(range(devices)))],
        tiled=True,
    )
    got = got.reshape(inp_count, time_count * tiles * 2, LANES)
    total_spectra = spec_local * time_count
    inputs = inp_count * local_inputs
    depth = 2 * total_spectra
    vmem = pl.BlockSpec(memory_space=pltpu.VMEM)
    return pl.pallas_call(
        lambda *refs: back_kernel(inputs // LANES, total_spectra, *refs),
        in_specs=[vmem] * 3,
        out_specs=pl.BlockSpec(memory_space=pl.ANY),
        out_shape=jax.ShapeDtypeStruct((1, inputs, inputs), jnp.bfloat16),
        scratch_shapes=[
            pltpu.VMEM((depth, inputs), jnp.bfloat16),
            pltpu.VMEM((inputs, depth), jnp.bfloat16),
            pltpu.VMEM((inputs, depth), jnp.bfloat16),
            pltpu.VMEM((inputs, inputs), jnp.bfloat16),
            pltpu.SemaphoreType.DMA((4,)),
        ],
        compiler_params=pltpu.CompilerParams(vmem_limit_bytes=24 * 1024 * 1024),
    )(got, jnp.asarray(fold_rows(time_count, tiles, tiles_local)), jnp.asarray(lane_turn()))


def solution(mesh):
    in_specs = (P("inp", "tm"),)
    out_specs = P(("inp", "tm"), None, None)
    return jax.shard_map(body, mesh=mesh, in_specs=in_specs, out_specs=out_specs, check_vma=False)
```

```python
import math

import jax
import jax.numpy as jnp
import ml_dtypes
import numpy as np
from jax import lax
from jax.experimental import pallas as pl
from jax.experimental.pallas import tpu as pltpu
from jax.sharding import PartitionSpec as P

NFFT = 2048
CHANNELS = 512
TAPS = 4
LANES = 128
WINDOW_ROWS = 512
TABLE_ROWS = 2048


def filter_window():
    sample = np.arange(TAPS * NFFT, dtype=np.float64) + 0.5
    shaped = np.sinc(sample / NFFT - TAPS / 2.0)
    tapered = 0.5 - 0.5 * np.cos(2.0 * math.pi * sample / (TAPS * NFFT))
    window = np.zeros((WINDOW_ROWS, NFFT), np.float32)
    window[:TAPS] = (shaped * tapered).reshape(TAPS, NFFT)
    return window


def phase_rows(block):
    sample = np.arange(NFFT // 4, dtype=np.int64)
    bin_index = NFFT // 2 - CHANNELS + np.arange(CHANNELS, dtype=np.int64)
    product = (bin_index[:, None] * sample[None, :]) % NFFT
    angle = (product.astype(np.float32) * np.float32(2.0 * math.pi / NFFT)).astype(np.float64)
    paired = np.stack([np.cos(angle), -np.sin(angle)]).astype(np.float32)
    paired = paired.reshape(2, block, 4, NFFT // 4).transpose(2, 0, 1, 3)[:, :, ::-1]
    table = np.zeros((TABLE_ROWS, NFFT // 4), ml_dtypes.bfloat16)
    table[: 2 * CHANNELS] = paired.reshape(2 * CHANNELS, NFFT // 4).astype(ml_dtypes.bfloat16)
    return table


def front_kernel(v_hbm, w_hbm, t_hbm, out_ref, v_ref, w_ref, t_ref, filt, stage, v_sem, w_sem, t_sem):
    inputs = v_ref.shape[0]
    spec_local = v_ref.shape[1] // NFFT
    per_tile = LANES // inputs
    tiles = filt.shape[0] // LANES
    block = t_ref.shape[0] // 8
    parts = v_sem.shape[0]
    width = v_ref.shape[1] // parts
    fetch_v = [
        pltpu.make_async_copy(
            v_hbm.at[:, i * width : (i + 1) * width], v_ref.at[:, i * width : (i + 1) * width], v_sem.at[i]
        )
        for i in range(parts)
    ]
    fetch_w = pltpu.make_async_copy(w_hbm.at[: w_ref.shape[0]], w_ref, w_sem)
    fetch_t = pltpu.make_async_copy(t_hbm.at[: t_ref.shape[0]], t_ref, t_sem)
    fetch_w.start()
    fetch_v[0].start()
    fetch_v[1].start()
    fetch_t.start()
    fetch_v[2].start()
    fetch_v[3].start()
    fetch_w.wait()

    def filter_tiles(first, last, off):
        weights = [w_ref[k : k + 1, pl.ds(off, LANES)] for k in range(TAPS)]
        slots = range(first * per_tile, last * per_tile)
        need = sorted({j + k - TAPS + 1 for j in slots for k in range(TAPS)} & set(range(spec_local)))
        rows = {
            s: v_ref[:, pl.ds(pl.multiple_of(s * NFFT + off, LANES), LANES)].astype(jnp.float32) for s in need
        }
        for j in slots:
            total = None
            for k in range(TAPS):
                s = j + k - TAPS + 1
                if s in rows:
                    term = weights[k] * rows[s]
                    total = term if total is None else total + term
            if total is None:
                total = jnp.zeros((inputs, LANES), jnp.float32)
            filt[j * inputs : (j + 1) * inputs, pl.ds(off, LANES)] = total.astype(jnp.bfloat16)

    def phases(residue):
        real = t_ref[2 * residue * block : (2 * residue + 1) * block, :]
        imag = t_ref[(2 * residue + 1) * block : (2 * residue + 2) * block, :]
        turns = [(real, imag), (imag, -real), (-real, -imag), (-imag, real)]
        quarters = [turns[(residue * q) % 4] for q in range(4)]
        return jnp.concatenate([jnp.concatenate([part[r] for part in quarters], axis=1) for r in range(2)], axis=0)

    def transform(first, last):
        for residue in range(0, 4, 2):
            acc = lax.dot_general(
                jnp.concatenate([phases(residue + d) for d in range(2)], axis=0),
                filt[first * LANES : last * LANES, :],
                (((1,), (1,)), ((), ())),
                preferred_element_type=jnp.float32,
            )
            for d in range(2):
                for t in range(first, last):
                    for r in range(2):
                        stage[pl.ds((3 - residue - d) * 2 * tiles + 2 * t + r, block, stride=8 * tiles), :] = acc[
                            (2 * d + r) * block : (2 * d + r + 1) * block, (t - first) * LANES : (t - first + 1) * LANES
                        ]

    fetch_v[0].wait()
    fetch_v[1].wait()

    @pl.loop(0, NFFT // LANES)
    def _(q):
        filter_tiles(0, 2, pl.multiple_of(q * LANES, LANES))

    fetch_v[2].wait()
    fetch_v[3].wait()
    fetch_t.wait()
    transform(0, 2)
    for q in range(NFFT // LANES):
        filter_tiles(2, 4, q * LANES)
    for q in range(NFFT // LANES):
        filter_tiles(4, tiles, q * LANES)
    transform(2, tiles)
    out_ref[...] = stage[...].astype(jnp.bfloat16)


def back_kernel(groups, total_spectra, x_ref, fold_ref, perm_ref, out_ref, a_ref, at_ref, bt_ref, stage, sems):
    inputs = groups * LANES
    half = LANES // 2
    for h in range(groups // 2):
        folded = []
        for g in (2 * h, 2 * h + 1):
            joined = jnp.concatenate([x_ref[4 * groups - 1 - 4 * g - i] for i in range(4)], axis=1)
            spectra = jnp.dot(fold_ref[...], joined, preferred_element_type=jnp.float32)
            folded.append(spectra.astype(jnp.bfloat16))
        turned = jnp.dot(
            jnp.concatenate(folded, axis=0), perm_ref[...], preferred_element_type=jnp.float32
        ).astype(jnp.bfloat16)
        for k in range(2):
            cols = slice((2 * h + k) * LANES, (2 * h + k + 1) * LANES)
            for u in range(4):
                rows = slice(u * LANES, (u + 1) * LANES)
                part = turned[k * LANES : (k + 1) * LANES, rows]
                a_ref[rows, cols] = part
                at_ref[cols, rows] = part.T
                bt_ref[cols, rows] = jnp.concatenate([part[half:], -part[:half]], axis=0).T
    scale = 1.0 / total_spectra
    wide = a_ref[...].astype(jnp.float32)
    row_gain = lax.rsqrt(jnp.sum(wide * wide, axis=0, keepdims=True) * scale + 1e-06) * scale
    size = inputs // 4
    copies = []
    for i in range(4):
        rows = slice(i * size, (i + 1) * size)
        tall = at_ref[rows, :].astype(jnp.float32)
        col_gain = lax.rsqrt(jnp.sum(tall * tall, axis=1, keepdims=True) * scale + 1e-06)
        upper = jnp.dot(at_ref[rows, :], a_ref[:, i * size :], preferred_element_type=jnp.float32)
        lower = jnp.dot(bt_ref[rows, :], a_ref[:, : (i + 1) * size], preferred_element_type=jnp.float32)
        keep = lax.broadcasted_iota(jnp.int32, (size, size), 0) <= lax.broadcasted_iota(jnp.int32, (size, size), 1)
        for j in range(4):
            cols = slice(j * size, (j + 1) * size)
            if j < i:
                part = lower[:, cols]
            elif j > i:
                part = upper[:, (j - i) * size : (j - i + 1) * size]
            else:
                part = jnp.where(keep, upper[:, :size], lower[:, cols])
            stage[rows, cols] = (part * col_gain * row_gain[:, cols]).astype(jnp.bfloat16)
        copies.append(pltpu.make_async_copy(stage.at[rows, :], out_ref.at[0, rows, :], sems.at[i]))
        copies[-1].start()
    for copy in copies:
        copy.wait()


def fold_rows(time_count, tiles, tiles_local):
    fold = np.zeros((2, time_count, tiles_local, time_count, tiles, 2), np.float32)
    for r in range(2):
        for t in range(time_count):
            for u in range(tiles_local):
                fold[r, t, u, t, u, r] = 1.0
            if t:
                fold[r, t, 0, t - 1, tiles_local, r] = 1.0
    return fold[:, :, :, ::-1].reshape(2 * time_count * tiles_local, -1).astype(ml_dtypes.bfloat16)


def lane_turn():
    turn = np.zeros((4, 4, 32, 4, 4, 32), np.float32)
    for i in range(4):
        for u in range(4):
            for a in range(32):
                turn[i, u, a, u, i, a] = 1.0
    return turn.reshape(512, 512).astype(ml_dtypes.bfloat16)


def body(voltages):
    inp_count = lax.axis_size("inp")
    time_count = lax.axis_size("tm")
    devices = inp_count * time_count
    local_inputs = voltages.shape[0]
    spec_local = voltages.shape[1] // NFFT
    slots = spec_local + 4
    tiles = slots * local_inputs // LANES
    tiles_local = spec_local * local_inputs // LANES
    block = CHANNELS // 4
    rows = CHANNELS * 2 * tiles
    hbm = pl.BlockSpec(memory_space=pl.ANY)
    sent = pl.pallas_call(
        front_kernel,
        in_specs=[hbm] * 3,
        out_specs=pl.BlockSpec(memory_space=pltpu.VMEM),
        out_shape=jax.ShapeDtypeStruct((rows, LANES), jnp.bfloat16),
        scratch_shapes=[
            pltpu.VMEM(voltages.shape, jnp.bfloat16),
            pltpu.VMEM((8, NFFT), jnp.float32),
            pltpu.VMEM((2 * CHANNELS, NFFT // 4), jnp.bfloat16),
            pltpu.VMEM((slots * local_inputs, NFFT), jnp.bfloat16),
            pltpu.VMEM((rows, LANES), jnp.float32),
            pltpu.SemaphoreType.DMA((4,)),
            pltpu.SemaphoreType.DMA,
            pltpu.SemaphoreType.DMA,
        ],
        compiler_params=pltpu.CompilerParams(vmem_limit_bytes=51 * 1024 * 1024),
    )(voltages, jnp.asarray(filter_window()), jnp.asarray(phase_rows(block)))
    got = lax.all_to_all(
        sent.reshape(devices, tiles, 2, LANES),
        ("inp", "tm"),
        split_axis=0,
        concat_axis=0,
        axis_index_groups=[list(reversed(range(devices)))],
        tiled=True,
    )
    got = got.reshape(inp_count, time_count * tiles * 2, LANES)
    total_spectra = spec_local * time_count
    inputs = inp_count * local_inputs
    depth = 2 * total_spectra
    vmem = pl.BlockSpec(memory_space=pltpu.VMEM)
    return pl.pallas_call(
        lambda *refs: back_kernel(inputs // LANES, total_spectra, *refs),
        in_specs=[vmem] * 3,
        out_specs=pl.BlockSpec(memory_space=pl.ANY),
        out_shape=jax.ShapeDtypeStruct((1, inputs, inputs), jnp.bfloat16),
        scratch_shapes=[
            pltpu.VMEM((depth, inputs), jnp.bfloat16),
            pltpu.VMEM((inputs, depth), jnp.bfloat16),
            pltpu.VMEM((inputs, depth), jnp.bfloat16),
            pltpu.VMEM((inputs, inputs), jnp.bfloat16),
            pltpu.SemaphoreType.DMA((4,)),
        ],
        compiler_params=pltpu.CompilerParams(vmem_limit_bytes=24 * 1024 * 1024),
    )(got, jnp.asarray(fold_rows(time_count, tiles, tiles_local)), jnp.asarray(lane_turn()))


def solution(mesh):
    in_specs = (P("inp", "tm"),)
    out_specs = P(("inp", "tm"), None, None)
    return jax.shard_map(body, mesh=mesh, in_specs=in_specs, out_specs=out_specs, check_vma=False)
```

```python
import math

import jax
import jax.numpy as jnp
import ml_dtypes
import numpy as np
from jax import lax
from jax.experimental import pallas as pl
from jax.experimental.pallas import tpu as pltpu
from jax.sharding import PartitionSpec as P

NFFT = 2048
CHANNELS = 512
TAPS = 4
LANES = 128
WINDOW_ROWS = 512
TABLE_ROWS = 2048


def filter_window():
    sample = np.arange(TAPS * NFFT, dtype=np.float64) + 0.5
    shaped = np.sinc(sample / NFFT - TAPS / 2.0)
    tapered = 0.5 - 0.5 * np.cos(2.0 * math.pi * sample / (TAPS * NFFT))
    window = np.zeros((WINDOW_ROWS, NFFT), np.float32)
    window[:TAPS] = (shaped * tapered).reshape(TAPS, NFFT)
    return window


def phase_rows(block):
    sample = np.arange(NFFT // 4, dtype=np.int64)
    bin_index = NFFT // 2 - CHANNELS + np.arange(CHANNELS, dtype=np.int64)
    product = (bin_index[:, None] * sample[None, :]) % NFFT
    angle = (product.astype(np.float32) * np.float32(2.0 * math.pi / NFFT)).astype(np.float64)
    paired = np.stack([np.cos(angle), -np.sin(angle)]).astype(np.float32)
    paired = paired.reshape(2, block, 4, NFFT // 4).transpose(2, 0, 1, 3)[:, :, ::-1]
    table = np.zeros((TABLE_ROWS, NFFT // 4), ml_dtypes.bfloat16)
    table[: 2 * CHANNELS] = paired.reshape(2 * CHANNELS, NFFT // 4).astype(ml_dtypes.bfloat16)
    return table


def front_kernel(v_hbm, w_hbm, t_hbm, out_ref, v_ref, w_ref, t_ref, filt, stage, v_sem, w_sem, t_sem):
    inputs = v_ref.shape[0]
    spec_local = v_ref.shape[1] // NFFT
    per_tile = LANES // inputs
    tiles = filt.shape[0] // LANES
    block = t_ref.shape[0] // 8
    parts = v_sem.shape[0]
    width = v_ref.shape[1] // parts
    fetch_v = [
        pltpu.make_async_copy(
            v_hbm.at[:, i * width : (i + 1) * width], v_ref.at[:, i * width : (i + 1) * width], v_sem.at[i]
        )
        for i in range(parts)
    ]
    fetch_w = pltpu.make_async_copy(w_hbm.at[: w_ref.shape[0]], w_ref, w_sem)
    fetch_t = pltpu.make_async_copy(t_hbm.at[: t_ref.shape[0]], t_ref, t_sem)
    fetch_w.start()
    fetch_v[0].start()
    fetch_v[1].start()
    fetch_t.start()
    fetch_v[2].start()
    fetch_v[3].start()
    fetch_w.wait()

    def filter_tiles(first, last, off):
        weights = [w_ref[k : k + 1, pl.ds(off, LANES)] for k in range(TAPS)]
        slots = range(first * per_tile, last * per_tile)
        need = sorted({j + k - TAPS + 1 for j in slots for k in range(TAPS)} & set(range(spec_local)))
        rows = {
            s: v_ref[:, pl.ds(pl.multiple_of(s * NFFT + off, LANES), LANES)].astype(jnp.float32) for s in need
        }
        for j in slots:
            total = None
            for k in range(TAPS):
                s = j + k - TAPS + 1
                if s in rows:
                    term = weights[k] * rows[s]
                    total = term if total is None else total + term
            if total is None:
                total = jnp.zeros((inputs, LANES), jnp.float32)
            filt[j * inputs : (j + 1) * inputs, pl.ds(off, LANES)] = total.astype(jnp.bfloat16)

    def phases(residue):
        real = t_ref[2 * residue * block : (2 * residue + 1) * block, :]
        imag = t_ref[(2 * residue + 1) * block : (2 * residue + 2) * block, :]
        turns = [(real, imag), (imag, -real), (-real, -imag), (-imag, real)]
        quarters = [turns[(residue * q) % 4] for q in range(4)]
        return jnp.concatenate([jnp.concatenate([part[r] for part in quarters], axis=1) for r in range(2)], axis=0)

    def transform(first, last):
        for residue in range(0, 4, 2):
            acc = lax.dot_general(
                jnp.concatenate([phases(residue + d) for d in range(2)], axis=0),
                filt[first * LANES : last * LANES, :],
                (((1,), (1,)), ((), ())),
                preferred_element_type=jnp.float32,
            )
            for d in range(2):
                for t in range(first, last):
                    for r in range(2):
                        stage[pl.ds((3 - residue - d) * 2 * tiles + 2 * t + r, block, stride=8 * tiles), :] = acc[
                            (2 * d + r) * block : (2 * d + r + 1) * block, (t - first) * LANES : (t - first + 1) * LANES
                        ]

    fetch_v[0].wait()
    fetch_v[1].wait()

    @pl.loop(0, NFFT // LANES)
    def _(q):
        filter_tiles(0, 2, pl.multiple_of(q * LANES, LANES))

    fetch_v[2].wait()
    fetch_v[3].wait()
    fetch_t.wait()
    transform(0, 2)
    for q in range(NFFT // LANES):
        filter_tiles(2, 4, q * LANES)
    for q in range(NFFT // LANES):
        filter_tiles(4, tiles, q * LANES)
    transform(2, tiles)
    out_ref[...] = stage[...].astype(jnp.bfloat16)


def back_kernel(groups, total_spectra, x_ref, fold_ref, perm_ref, out_ref, a_ref, at_ref, bt_ref, stage, sems):
    inputs = groups * LANES
    half = LANES // 2
    for h in range(groups // 4):
        folded = []
        for g in range(4 * h, 4 * h + 4):
            joined = jnp.concatenate([x_ref[4 * groups - 1 - 4 * g - i] for i in range(4)], axis=1)
            spectra = jnp.dot(fold_ref[...], joined, preferred_element_type=jnp.float32)
            folded.append(spectra.astype(jnp.bfloat16))
        turned = jnp.dot(
            jnp.concatenate(folded, axis=0), perm_ref[...], preferred_element_type=jnp.float32
        ).astype(jnp.bfloat16)
        for k in range(4):
            cols = slice((4 * h + k) * LANES, (4 * h + k + 1) * LANES)
            for u in range(4):
                rows = slice(u * LANES, (u + 1) * LANES)
                part = turned[k * LANES : (k + 1) * LANES, rows]
                a_ref[rows, cols] = part
                at_ref[cols, rows] = part.T
                bt_ref[cols, rows] = jnp.concatenate([part[half:], -part[:half]], axis=0).T
    scale = 1.0 / total_spectra
    wide = a_ref[...].astype(jnp.float32)
    row_gain = lax.rsqrt(jnp.sum(wide * wide, axis=0, keepdims=True) * scale + 1e-06) * scale
    size = inputs // 4
    copies = []
    for i in range(4):
        rows = slice(i * size, (i + 1) * size)
        tall = at_ref[rows, :].astype(jnp.float32)
        col_gain = lax.rsqrt(jnp.sum(tall * tall, axis=1, keepdims=True) * scale + 1e-06)
        upper = jnp.dot(at_ref[rows, :], a_ref[:, i * size :], preferred_element_type=jnp.float32)
        lower = jnp.dot(bt_ref[rows, :], a_ref[:, : (i + 1) * size], preferred_element_type=jnp.float32)
        keep = lax.broadcasted_iota(jnp.int32, (size, size), 0) <= lax.broadcasted_iota(jnp.int32, (size, size), 1)
        for j in range(4):
            cols = slice(j * size, (j + 1) * size)
            if j < i:
                part = lower[:, cols]
            elif j > i:
                part = upper[:, (j - i) * size : (j - i + 1) * size]
            else:
                part = jnp.where(keep, upper[:, :size], lower[:, cols])
            stage[rows, cols] = (part * col_gain * row_gain[:, cols]).astype(jnp.bfloat16)
        copies.append(pltpu.make_async_copy(stage.at[rows, :], out_ref.at[0, rows, :], sems.at[i]))
        copies[-1].start()
    for copy in copies:
        copy.wait()


def fold_rows(time_count, tiles, tiles_local):
    fold = np.zeros((2, time_count, tiles_local, time_count, tiles, 2), np.float32)
    for r in range(2):
        for t in range(time_count):
            for u in range(tiles_local):
                fold[r, t, u, t, u, r] = 1.0
            if t:
                fold[r, t, 0, t - 1, tiles_local, r] = 1.0
    return fold[:, :, :, ::-1].reshape(2 * time_count * tiles_local, -1).astype(ml_dtypes.bfloat16)


def lane_turn():
    turn = np.zeros((4, 4, 32, 4, 4, 32), np.float32)
    for i in range(4):
        for u in range(4):
            for a in range(32):
                turn[i, u, a, u, i, a] = 1.0
    return turn.reshape(512, 512).astype(ml_dtypes.bfloat16)


def body(voltages):
    inp_count = lax.axis_size("inp")
    time_count = lax.axis_size("tm")
    devices = inp_count * time_count
    local_inputs = voltages.shape[0]
    spec_local = voltages.shape[1] // NFFT
    slots = spec_local + 4
    tiles = slots * local_inputs // LANES
    tiles_local = spec_local * local_inputs // LANES
    block = CHANNELS // 4
    rows = CHANNELS * 2 * tiles
    hbm = pl.BlockSpec(memory_space=pl.ANY)
    sent = pl.pallas_call(
        front_kernel,
        in_specs=[hbm] * 3,
        out_specs=pl.BlockSpec(memory_space=pltpu.VMEM),
        out_shape=jax.ShapeDtypeStruct((rows, LANES), jnp.bfloat16),
        scratch_shapes=[
            pltpu.VMEM(voltages.shape, jnp.bfloat16),
            pltpu.VMEM((8, NFFT), jnp.float32),
            pltpu.VMEM((2 * CHANNELS, NFFT // 4), jnp.bfloat16),
            pltpu.VMEM((slots * local_inputs, NFFT), jnp.bfloat16),
            pltpu.VMEM((rows, LANES), jnp.float32),
            pltpu.SemaphoreType.DMA((4,)),
            pltpu.SemaphoreType.DMA,
            pltpu.SemaphoreType.DMA,
        ],
        compiler_params=pltpu.CompilerParams(vmem_limit_bytes=51 * 1024 * 1024),
    )(voltages, jnp.asarray(filter_window()), jnp.asarray(phase_rows(block)))
    got = lax.all_to_all(
        sent.reshape(devices, tiles, 2, LANES),
        ("inp", "tm"),
        split_axis=0,
        concat_axis=0,
        axis_index_groups=[list(reversed(range(devices)))],
        tiled=True,
    )
    got = got.reshape(inp_count, time_count * tiles * 2, LANES)
    total_spectra = spec_local * time_count
    inputs = inp_count * local_inputs
    depth = 2 * total_spectra
    vmem = pl.BlockSpec(memory_space=pltpu.VMEM)
    return pl.pallas_call(
        lambda *refs: back_kernel(inputs // LANES, total_spectra, *refs),
        in_specs=[vmem] * 3,
        out_specs=pl.BlockSpec(memory_space=pl.ANY),
        out_shape=jax.ShapeDtypeStruct((1, inputs, inputs), jnp.bfloat16),
        scratch_shapes=[
            pltpu.VMEM((depth, inputs), jnp.bfloat16),
            pltpu.VMEM((inputs, depth), jnp.bfloat16),
            pltpu.VMEM((inputs, depth), jnp.bfloat16),
            pltpu.VMEM((inputs, inputs), jnp.bfloat16),
            pltpu.SemaphoreType.DMA((4,)),
        ],
        compiler_params=pltpu.CompilerParams(vmem_limit_bytes=24 * 1024 * 1024),
    )(got, jnp.asarray(fold_rows(time_count, tiles, tiles_local)), jnp.asarray(lane_turn()))


def solution(mesh):
    in_specs = (P("inp", "tm"),)
    out_specs = P(("inp", "tm"), None, None)
    return jax.shard_map(body, mesh=mesh, in_specs=in_specs, out_specs=out_specs, check_vma=False)
```
